128 devices in a mesh: section: 16 (over x_lo, z, core), expert: 8 (over y, x_hi).
Axes of the slice: x: 4 (x_hi: 2, x_lo: 2; x = x_hi * 2 + x_lo), y: 4, z: 4, core: 2. Of those that a mesh axis runs over, the one named last changes fastest.
Arguments:
- acts: bfloat16 [16, 512, 6144], P('section', 'expert'), may hold values from -6 to 6
- norm_gain: float32 [16, 6144], P('section'), may hold values from 0.1 to 1.9
- w_gate: bfloat16 [16, 8, 6144, 640], P('section', 'expert'), may hold values from -0.078125 to 0.078125
- w_up: bfloat16 [16, 8, 6144, 640], P('section', 'expert'), may hold values from -0.078125 to 0.078125
- w_down: bfloat16 [16, 8, 640, 6144], P('section', 'expert'), may hold values from -0.25 to 0.25
- routes: int32 [4, 16, 512, 4], P(None, 'section', 'expert'), may hold values from 0 to 7, all different within a row; in each aligned block of 64 rows (0 to 63, 64 to 127, ..., all dimensions but the last counted through in order) at most 48 rows name the same one
- gates: float32 [4, 16, 512, 4], P(None, 'section', 'expert'), may hold values from 0.2 to 1
Outputs:
- final_acts: bfloat16 [16, 512, 6144], P('section', 'expert')
The draws below stay inside these ranges and needn't reach their ends.
Inputs may be any that keep to these rules, and one draw needn't show every extreme that they name: `routes`: each row names 4 different experts. Within the rows of one device for one tick no expert is named by more than 48 rows, a bound that some block reaches.
All inputs are finite; a program needn't handle non-finite values.
Results may differ from the reference program's by a relative error of at most 0.02.
Values may be sent and summed in bfloat16 or wider, within the bound.
No kernel may reach another device: no remote copies, remote signals or barrier semaphores. Data moves between devices by JAX's collectives and lax.ppermute only.
A program may use at most 128 MiB of HBM per device.

```python
import math
import jax
import jax.numpy as jnp
import numpy as np
from jax import lax

D = 6144
EXPERTS = 8
TOP = 4
FF_DEV = 640
TOK_DEV = 64
TICKS = 4
CAP = 48
SECTIONS = 16
TOKENS_ST = 512


def block_scale(key, extent, shards, least, high):
    level = 1.0
    for axis_at, parts in shards:
        steps = jax.random.uniform(jax.random.fold_in(jax.random.fold_in(key, 6), axis_at), (parts,), jnp.float32, least / len(shards), high / len(shards))
        level = level * jnp.repeat(jnp.exp(steps), extent[axis_at] // parts).reshape((-1,) + (1,) * (len(extent) - 1 - axis_at))
    return level


def routed_block(own_key, own, number, rows, count, top, most, lean):
    ranking = jax.random.permutation(own_key, count)
    packed, usual = portions_of(count, rows * top, most, lean, True), portions_of(count, rows * top, most, lean, False)
    places = jnp.arange(count)

    def named(tallies, turn):
        used = int((tallies > 0).sum())
        fixed = max(1, used // 4)
        passed = fixed + (places - fixed + turn * (used - fixed)) % max(1, count - fixed)
        return jnp.zeros((count,), jnp.int32).at[ranking[jnp.where(places < fixed, places, passed)]].set(jnp.asarray(tallies, jnp.int32))

    tallies = jnp.where(number % 4 == 0, named(packed, number // 4), named(usual, number - number // 4 - 1))
    mixed = jax.random.permutation(jax.random.fold_in(own, 3), count)
    donor, taker = mixed[0:count // 2 * 2:2], mixed[1:count // 2 * 2:2]
    slack = jnp.minimum(tallies[donor] - 1, most - tallies[taker]) // 2
    slack = jnp.where((donor == ranking[0]) | (taker == ranking[0]) | (tallies[taker] == 0), 0, jnp.maximum(slack, 0))
    passed = jax.random.randint(jax.random.fold_in(own, 4), (count // 2,), 0, 1 << 20) % (slack + 1)
    tallies = tallies.at[donor].add(-passed).at[taker].add(passed)
    members = jnp.searchsorted(jnp.cumsum(tallies), jnp.arange(rows * top), side="right").astype(jnp.int32)
    table = members.reshape(top, rows).T
    table = table[jax.random.permutation(jax.random.fold_in(own, 1), rows)]
    turn = jax.random.randint(jax.random.fold_in(own, 2), (rows, 1), 0, top)
    return jnp.take_along_axis(table, (jnp.arange(top)[None, :] + turn) % top, axis=1)


def portions_of(amount, total, reach, skew, full):
    portions = [(1 << 20) // math.isqrt(standing ** skew) + 1 for standing in range(1, amount + 1)]
    largest = reach if full else min(reach, max(-(-total // amount), total * portions[0] // sum(portions)))
    least = 1 if total - largest >= amount - 1 else 0
    counts, spare = [largest] + [least] * (amount - 1), total - largest - least * (amount - 1)
    while spare > 0:
        movable = [i for i in range(1, amount) if counts[i] < largest] or [i for i in range(1, amount) if counts[i] < reach]
        pool, remaining = sum([portions[i] for i in movable]), spare
        for i in movable:
            more = min(reach - counts[i], max(1, remaining * portions[i] // pool), spare)
            counts[i] = counts[i] + more
            spare = spare - more
    return np.array(counts)


def bell_draw(own_key, extent, spread, limit, shards=(), held_as=jnp.bfloat16):
    values = spread * jax.random.normal(own_key, extent, jnp.float32)
    if shards:
        values = values * block_scale(own_key, extent, shards, -0.22, 0.18)
    return jnp.clip(values, -limit, limit).astype(held_as)


def setup_inputs(seed: int = 0) -> dict:
    splits = jax.random.split(jax.random.key(seed), 8)
    acts = bell_draw(splits[0], (SECTIONS, TOKENS_ST, D), 1.0, 6.0, ((0, 16), (1, 8)))
    norm_gain = jnp.clip(1.0 + 0.18 * jax.random.normal(splits[1], (SECTIONS, D), jnp.float32), 0.1, 1.9)
    w_gate = bell_draw(splits[2], (SECTIONS, EXPERTS, D, FF_DEV), D ** -0.5, 0.078125, ((0, 16), (1, 8)))
    w_up = bell_draw(splits[3], (SECTIONS, EXPERTS, D, FF_DEV), D ** -0.5, 0.078125, ((0, 16), (1, 8)))
    w_down = bell_draw(splits[4], (SECTIONS, EXPERTS, FF_DEV, D), FF_DEV ** -0.5, 0.25, ((0, 16), (1, 8)))
    routes_keys = jax.random.split(jax.random.fold_in(splits[5], 1), TICKS * SECTIONS * TOKENS_ST // TOK_DEV)
    routes_turns = jax.random.permutation(jax.random.fold_in(splits[5], 3), TICKS * SECTIONS * TOKENS_ST // TOK_DEV)
    routes = jax.vmap(lambda own, number: routed_block(jax.random.fold_in(splits[5], 2), own, number, TOK_DEV, EXPERTS, TOP, CAP, 2))(routes_keys, routes_turns).reshape((TICKS, SECTIONS, TOKENS_ST, TOP))
    gates = jnp.clip(0.2 + 0.8 * jax.random.uniform(splits[6], (TICKS, SECTIONS, TOKENS_ST, TOP), jnp.float32) ** block_scale(splits[6], (TICKS, SECTIONS, TOKENS_ST, TOP), ((1, 16), (2, 8)), -0.2, 0.2), 0.2, 1.0)
    return {"acts": acts, "norm_gain": norm_gain, "w_gate": w_gate, "w_up": w_up, "w_down": w_down, "routes": routes, "gates": gates}


def normalize(rows, gain):
    values = rows.astype(jnp.float32)
    meansq = lax.optimization_barrier(jnp.mean(values * values, axis=-1, keepdims=True))
    return (values * lax.rsqrt(meansq + 1e-05) * gain.astype(jnp.float32)[None, :]).astype(jnp.bfloat16)

def layer(items):
    rows, gain, gate_w, up_w, down_w, route, gate = items
    normed = normalize(rows, gain)
    expert_ids = jnp.arange(EXPERTS, dtype=jnp.int32)
    weights = lax.optimization_barrier(jnp.sum(gate[:, :, None] * (route[:, :, None] == expert_ids[None, None, :]).astype(jnp.float32), axis=1))

    def one_expert(total, pieces):
        gate_e, up_e, down_e, index = pieces
        gated = jnp.dot(normed, gate_e, preferred_element_type=jnp.float32)
        upper = jnp.dot(normed, up_e, preferred_element_type=jnp.float32)
        hidden = (jax.nn.silu(gated) * upper).astype(jnp.bfloat16)
        output = jnp.dot(hidden, down_e, preferred_element_type=jnp.float32).astype(jnp.bfloat16)
        column = lax.dynamic_slice_in_dim(weights, index, 1, 1)
        return (total + column * output.astype(jnp.float32), None)
    start = jnp.zeros(rows.shape, jnp.float32)
    total, unused = lax.scan(one_expert, start, (gate_w, up_w, down_w, expert_ids))
    return (rows.astype(jnp.float32) + total).astype(jnp.bfloat16)

def reference(acts, norm_gain, w_gate, w_up, w_down, routes, gates):
    state = acts
    for tick in range(TICKS):
        state = lax.map(layer, (state, norm_gain, w_gate, w_up, w_down, routes[tick], gates[tick]))
        state = jnp.roll(state, 1, axis=0)
    return state
```

```python
import functools

import jax
import jax.numpy as jnp
from jax import lax
from jax.experimental import pallas as pl
from jax.experimental.pallas import tpu as pltpu
from jax.sharding import PartitionSpec as P

TICKS = 4
STREAMS = 1
FIRST = 3584
DEEP = 1024
WIDE = 1024
RINGS = [[0, 2, 4, 6], [1, 3, 5, 7]]


def relayed(value):
    return lax.ppermute(value, "section", [(i, (i + 1) % 16) for i in range(16)])


def relayed_across(value):
    pairs = [(s * 8 + e, ((s + 1) % 16) * 8 + (e ^ 1)) for s in range(16) for e in range(8)]
    return lax.ppermute(value, ("section", "expert"), pairs)


def across(value):
    return lax.ppermute(value, "expert", [(i, i ^ 1) for i in range(8)])


def upward(value):
    return lax.ppermute(value, "expert", [(i, (i + 2) % 8) for i in range(8)])


def downward(value):
    return lax.ppermute(value, "expert", [(i, (i - 2) % 8) for i in range(8)])


def plus(*terms):
    total = terms[0].astype(jnp.float32)
    for term in terms[1:]:
        total = total + term.astype(jnp.float32)
    return total


def normalize(first, second, gain):
    split = first.shape[1]
    one, two = first.astype(jnp.float32), second.astype(jnp.float32)
    total = jnp.sum(one * one, axis=-1, keepdims=True) + jnp.sum(two * two, axis=-1, keepdims=True)
    scale = lax.rsqrt(total / gain.shape[0] + 1e-05)
    one = (one * scale * gain[None, :split]).astype(jnp.bfloat16)
    two = (two * scale * gain[None, split:]).astype(jnp.bfloat16)
    return one, two


def gather(first, second):
    half = first.shape[1] // 2
    near = lax.all_gather(second, "expert", axis=0, axis_index_groups=RINGS)
    other = across(first)
    own_l = jnp.concatenate([first[:, :half], other[:, :half]], axis=0)
    own_r = jnp.concatenate([first[:, half:], other[:, half:]], axis=0)
    below_l, above_r = upward(own_l), downward(own_r)
    below_r, above_l = upward(own_r), downward(own_l)
    opp_l, opp_r = upward(below_l), downward(above_r)
    far = across(near)
    return (own_l, own_r, below_l, below_r, above_l, above_r, opp_l, opp_r), (near, far)


def scatter_sum(pieces, near, far, rows):
    own_l, own_r, below_l, below_r, above_l, above_r, opp_l, opp_r = pieces
    other = across(far)
    arrived_l, arrived_r = upward(opp_l), downward(opp_r)
    sum_r, sum_l = upward(above_r), downward(below_l)
    both = plus(near, other).astype(jnp.bfloat16)
    second = lax.psum_scatter(both, "expert", scatter_dimension=0, axis_index_groups=RINGS)
    above_l = plus(above_l, arrived_l).astype(jnp.bfloat16)
    below_r = plus(below_r, arrived_r).astype(jnp.bfloat16)
    top_l, low_r = upward(above_l), downward(below_r)
    left = plus(own_l, sum_l, top_l)
    right = plus(own_r, sum_r, low_r)
    return jnp.concatenate([left, right], axis=1), second


def mlp_kernel(split, rows, me_ref, weight_ref, gate_ref, up_ref, down_ref, *refs):
    pieces, (near, far) = refs[:8], refs[8:10]
    out_pieces, (out_near, out_far) = refs[10:18], refs[18:20]
    inputs, gated, upper, hidden = refs[20:]
    step = pl.program_id(0)
    half = split // 2
    width = inputs.shape[1]
    deep_steps = width // DEEP
    wide_steps = width // WIDE
    high, low = me_ref[0] // 2, me_ref[0] % 2

    def place(dy, dx):
        slot = lax.rem(high + dy, 4) * 2 + lax.rem(low + dx, 2)
        return pl.ds(pl.multiple_of(slot * rows, rows), rows)

    turns = (0, 3, 1, 2)

    @pl.when(step == 0)
    def _():
        for at in range(8):
            dy, side = turns[at // 2], at % 2
            for dx in range(2):
                inputs[place(dy, dx), side * half : (side + 1) * half] = pieces[at][dx * rows : (dx + 1) * rows, :]
        for y in range(4):
            for dx, source in ((0, near), (1, far)):
                slot = 2 * y + lax.rem(low + dx, 2)
                inputs[pl.ds(pl.multiple_of(slot * rows, rows), rows), split:] = source[y]
        gated[...] = jnp.zeros_like(gated)
        upper[...] = jnp.zeros_like(upper)

    @pl.when(step < deep_steps)
    def _():
        block = inputs[:, pl.ds(pl.multiple_of(step * DEEP, DEEP), DEEP)]
        gated[...] += jnp.dot(block, gate_ref[...], preferred_element_type=jnp.float32)
        upper[...] += jnp.dot(block, up_ref[...], preferred_element_type=jnp.float32)

    @pl.when(step == deep_steps - 1)
    def _():
        value = gated[...]
        hidden[...] = (value / (1.0 + jnp.exp(-value)) * upper[...]).astype(jnp.bfloat16)

    @pl.when(step >= deep_steps)
    def _():
        at = step - deep_steps
        output = jnp.dot(hidden[...], down_ref[...], preferred_element_type=jnp.float32)
        output = (output * weight_ref[...]).astype(jnp.bfloat16)
        inputs[:, pl.ds(pl.multiple_of(at * WIDE, WIDE), WIDE)] = output

    @pl.when(step == deep_steps + wide_steps - 1)
    def _():
        for at in range(8):
            dy, side = turns[at // 2], at % 2
            for dx in range(2):
                out_pieces[at][dx * rows : (dx + 1) * rows, :] = inputs[place(dy, dx), side * half : (side + 1) * half]
        for y in range(4):
            for dx, target in ((0, out_near), (1, out_far)):
                slot = 2 * y + lax.rem(low + dx, 2)
                target[y] = inputs[pl.ds(pl.multiple_of(slot * rows, rows), rows), split:]


def expert(me, weight, gate_w, up_w, down_w, pieces, near, far):
    width, inner = gate_w.shape
    rows = near.shape[1]
    total = rows * 8
    split = pieces[0].shape[1] * 2
    deep_steps, wide_steps = width // DEEP, width // WIDE
    whole = pl.BlockSpec(memory_space=pltpu.VMEM)
    shapes = [jax.ShapeDtypeStruct(p.shape, jnp.bfloat16) for p in (*pieces, near, far)]
    outs = pl.pallas_call(
        functools.partial(mlp_kernel, split, rows),
        grid=(deep_steps + wide_steps,),
        in_specs=[
            pl.BlockSpec(memory_space=pltpu.SMEM),
            whole,
            pl.BlockSpec((DEEP, inner), lambda i: (jnp.minimum(i, deep_steps - 1), 0)),
            pl.BlockSpec((DEEP, inner), lambda i: (jnp.minimum(i, deep_steps - 1), 0)),
            pl.BlockSpec((inner, WIDE), lambda i: (0, jnp.maximum(i - deep_steps, 0))),
        ]
        + [whole] * 10,
        out_specs=[whole] * 10,
        out_shape=shapes,
        scratch_shapes=[
            pltpu.VMEM((total, width), jnp.bfloat16),
            pltpu.VMEM((total, inner), jnp.float32),
            pltpu.VMEM((total, inner), jnp.float32),
            pltpu.VMEM((total, inner), jnp.bfloat16),
        ],
        compiler_params=pltpu.CompilerParams(
            dimension_semantics=("arbitrary",), vmem_limit_bytes=44 * 1024 * 1024
        ),
        cost_estimate=pl.CostEstimate(
            flops=6 * total * width * inner,
            bytes_accessed=6 * width * inner + 4 * total * width,
            transcendentals=total * inner,
        ),
        name="expert_mlp",
    )(me, weight, gate_w, up_w, down_w, *pieces, near, far)
    return outs[:8], outs[8], outs[9]


def body(acts, norm_gain, w_gate, w_up, w_down, routes, gates):
    gain = norm_gain[0]
    gate_w, up_w, down_w = w_gate[0, 0], w_up[0, 0], w_down[0, 0]
    tok_rows = acts.shape[1]
    rows = tok_rows // STREAMS
    me = lax.axis_index("expert")
    ids = jnp.arange(8, dtype=jnp.int32)
    chosen = (routes[:, 0, :, :, None] == ids).astype(jnp.float32)
    weights = jnp.sum(gates[:, 0, :, :, None] * chosen, axis=2)
    weights = jnp.transpose(weights, (2, 0, 1)).reshape(8, TICKS * tok_rows)
    weights = lax.all_to_all(weights, "expert", split_axis=0, concat_axis=0, tiled=True)
    weights = weights.reshape(8, TICKS, tok_rows)
    me = jnp.reshape(me, (1,)).astype(jnp.int32)
    states = [
        (acts[0, i * rows : (i + 1) * rows, :FIRST], acts[0, i * rows : (i + 1) * rows, FIRST:])
        for i in range(STREAMS)
    ]
    for tick in range(TICKS):
        done = []
        for stream, (first, second) in enumerate(states):
            pieces, (near, far) = gather(*normalize(first, second, gain))
            weight = weights[:, tick, stream * rows : (stream + 1) * rows].reshape(8 * rows, 1)
            pieces, near, far = expert(me, weight, gate_w, up_w, down_w, pieces, near, far)
            sums, more = scatter_sum(pieces, near, far, rows)
            kept = relayed((first.astype(jnp.float32) + sums[:rows]).astype(jnp.bfloat16))
            sent = relayed_across(sums[rows:].astype(jnp.bfloat16))
            second = relayed(plus(second, more).astype(jnp.bfloat16))
            done.append((plus(kept, sent).astype(jnp.bfloat16), second))
        states = done
    return jnp.concatenate([jnp.concatenate(state, axis=1) for state in states], axis=0)[None]


def solution(mesh):
    return jax.shard_map(
        body,
        mesh=mesh,
        in_specs=(
            P("section", "expert", None),
            P("section", None),
            P("section", "expert", None, None),
            P("section", "expert", None, None),
            P("section", "expert", None, None),
            P(None, "section", "expert", None),
            P(None, "section", "expert", None),
        ),
        out_specs=P("section", "expert", None),
        check_vma=False,
    )
```

```python
import functools

import jax
import jax.numpy as jnp
from jax import lax
from jax.experimental import pallas as pl
from jax.experimental.pallas import tpu as pltpu
from jax.sharding import PartitionSpec as P

TICKS = 4
FIRST = 4096
DEEP = 1024
WIDE = 2048
SLOTS = 4
RINGS = [[0, 2, 4, 6], [1, 3, 5, 7]]
LIMIT = 38


def relayed(value, turn):
    pairs = []
    for s in range(16):
        for e in range(8):
            target = e ^ 1 if turn is None else (e + turn) % 8
            pairs.append((s * 8 + e, (s + 1) % 16 * 8 + target))
    return lax.ppermute(value, ("section", "expert"), pairs)


def across(value):
    return lax.ppermute(value, "expert", [(i, i ^ 1) for i in range(8)])


def upward(value):
    return lax.ppermute(value, "expert", [(i, (i + 2) % 8) for i in range(8)])


def downward(value):
    return lax.ppermute(value, "expert", [(i, (i - 2) % 8) for i in range(8)])


def plus(*terms):
    total = terms[0].astype(jnp.float32)
    for term in terms[1:]:
        total = total + term.astype(jnp.float32)
    return total


def normalize(first, second, gain):
    split = first.shape[1]
    one, two = first.astype(jnp.float32), second.astype(jnp.float32)
    total = jnp.sum(one * one, axis=-1, keepdims=True) + jnp.sum(two * two, axis=-1, keepdims=True)
    scale = lax.rsqrt(total / gain.shape[0] + 1e-05)
    one = (one * scale * gain[None, :split]).astype(jnp.bfloat16)
    two = (two * scale * gain[None, split:]).astype(jnp.bfloat16)
    return one, two


def thirds(weights):
    high = lax.reduce_precision(weights, 8, 7)
    rest = weights - high
    middle = lax.reduce_precision(rest, 8, 7)
    parts = jnp.concatenate([high, middle, rest - middle], axis=1)
    return jnp.pad(parts, ((0, 0), (0, 128 - parts.shape[1]))).astype(jnp.bfloat16)


def whole_again(parts):
    size = TICKS * 8
    high, middle, low = (parts[:, i * size : (i + 1) * size].astype(jnp.float32) for i in range(3))
    return high + (middle + low)


def gather(first, second):
    half, quarter = first.shape[1] // 2, second.shape[1] // 256 * 128
    other = across(first)
    below, above = upward(second), downward(second)
    own_l = jnp.concatenate([first[:, :half], other[:, :half]], axis=0)
    own_r = jnp.concatenate([first[:, half:], other[:, half:]], axis=0)
    below_l, above_r = upward(own_l), downward(own_r)
    below_r, above_l = upward(own_r), downward(own_l)
    facing = jnp.concatenate([upward(below[:, :quarter]), downward(above[:, quarter:])], axis=1)
    near = jnp.concatenate([second, below, above, facing], axis=0)
    far = across(after(near, other))
    opp_l, opp_r = upward(below_l), downward(above_r)
    return (own_l, own_r, below_l, below_r, above_l, above_r, opp_l, opp_r), near, far


def after(value, *others):
    return lax.optimization_barrier((value, *others))[0]


def scatter_first(first, pieces):
    own_l, own_r, below_l, below_r, above_l, above_r, opp_l, opp_r = pieces
    rows = first.shape[0]
    arrived_l, arrived_r = upward(opp_l), downward(opp_r)
    sum_r, sum_l = upward(above_r), downward(below_l)
    top_l = upward(plus(above_l, arrived_l).astype(jnp.bfloat16))
    low_r = downward(plus(below_r, arrived_r).astype(jnp.bfloat16))
    sums = jnp.concatenate([plus(own_l, sum_l, top_l), plus(own_r, sum_r, low_r)], axis=1)
    sent = relayed(sums[rows:].astype(jnp.bfloat16), None)
    kept = relayed((first.astype(jnp.float32) + sums[:rows]).astype(jnp.bfloat16), 0)
    return plus(kept, sent).astype(jnp.bfloat16)


def scatter_second(second, near, far):
    both = plus(near, across(far)).astype(jnp.bfloat16)
    total = lax.psum_scatter(both, "expert", scatter_dimension=0, axis_index_groups=RINGS)
    return relayed(plus(second, total).astype(jnp.bfloat16), 0)


def accumulate(acc, rows, gate_ref, up_ref, first):
    inner = gate_ref.shape[1]
    for at, ref in ((0, gate_ref), (inner, up_ref)):
        columns = slice(at, at + inner)
        part = jnp.dot(rows, ref[...], preferred_element_type=jnp.float32)
        acc[:, columns] = part if first else acc[:, columns] + part


def mlp_kernel(turns, weight, gate_hbm, up_hbm, down_hbm, *refs):
    pieces, (near, far) = refs[:8], refs[8:10]
    outs, (out_near, out_far) = refs[10:18], refs[18:20]
    gates, ups, downs, acc, hidden, in_sems, out_sems = refs[20:]
    pair, half = pieces[0].shape
    rows = pair // 2
    inner = hidden.shape[1]
    steps = gate_hbm.shape[0] // DEEP
    wides = down_hbm.shape[1] // WIDE

    def fetch(at):
        slot, span = at % SLOTS, pl.ds(at * DEEP, DEEP)
        return (
            pltpu.make_async_copy(gate_hbm.at[span, :], gates.at[slot], in_sems.at[0, slot]),
            pltpu.make_async_copy(up_hbm.at[span, :], ups.at[slot], in_sems.at[1, slot]),
        )

    def fetch_down(at):
        return pltpu.make_async_copy(down_hbm.at[:, pl.ds(at * WIDE, WIDE)], downs.at[at], out_sems.at[at])

    def start(at):
        for copy in fetch(at):
            copy.start()

    def wait(at):
        for copy in fetch(at):
            copy.wait()

    def block(at):
        start = at * DEEP
        if start < 2 * half:
            side, columns = start // half, pl.ds(start % half, DEEP)
            return jnp.concatenate([pieces[2 * dy + side][:, columns] for dy in range(4)], axis=0)
        columns = pl.ds(start - 2 * half, DEEP)
        parts = [ref[dy * rows : (dy + 1) * rows, columns] for dy in range(4) for ref in (near, far)]
        return jnp.concatenate(parts, axis=0)

    for at in range(SLOTS):
        start(at)
    for at in range(steps):
        wait(at)
        accumulate(acc, block(at), gates.at[at % SLOTS], ups.at[at % SLOTS], at == 0)
        if at + SLOTS < steps:
            start(at + SLOTS)
        elif at + SLOTS == steps:
            for wide in range(wides):
                fetch_down(wide).start()
    scale = weight[...]
    value = acc[:, :inner]
    hidden[...] = (value / (1.0 + jnp.exp(-value)) * acc[:, inner:] * scale).astype(jnp.bfloat16)
    for at in range(wides):
        fetch_down(at).wait()
        for part in range(0, WIDE, 512):
            down = downs[at, :, part : part + 512]
            output = jnp.dot(hidden[...], down, preferred_element_type=jnp.float32).astype(jnp.bfloat16)
            start_at = at * WIDE + part
            if start_at < 2 * half:
                side, columns = start_at // half, pl.ds(start_at % half, 512)
                for dy in range(4):
                    outs[2 * dy + side][:, columns] = output[dy * pair : (dy + 1) * pair, :]
            else:
                columns = pl.ds(start_at - 2 * half, 512)
                for dy in range(4):
                    out_near[turns[dy], :, columns] = output[2 * dy * rows : (2 * dy + 1) * rows, :]
                    out_far[turns[dy], :, columns] = output[(2 * dy + 1) * rows : (2 * dy + 2) * rows, :]


def expert(turns, weight, gate_w, up_w, down_w, pieces, near, far):
    width, inner = gate_w.shape
    total = pieces[0].shape[0] * 4
    wides = width // WIDE
    mixed = (4, total // 8, width - 2 * pieces[0].shape[1])
    whole = pl.BlockSpec(memory_space=pltpu.VMEM)
    outs = pl.pallas_call(
        mlp_kernel,
        in_specs=[pl.BlockSpec(memory_space=pltpu.SMEM), whole] + [pl.BlockSpec(memory_space=pltpu.HBM)] * 3 + [whole] * 10,
        out_specs=[whole] * 10,
        out_shape=[jax.ShapeDtypeStruct(p.shape, jnp.bfloat16) for p in pieces]
        + [jax.ShapeDtypeStruct(mixed, jnp.bfloat16)] * 2,
        scratch_shapes=[
            pltpu.VMEM((SLOTS, DEEP, inner), jnp.bfloat16),
            pltpu.VMEM((SLOTS, DEEP, inner), jnp.bfloat16),
            pltpu.VMEM((wides, inner, WIDE), jnp.bfloat16),
            pltpu.VMEM((total, 2 * inner), jnp.float32),
            pltpu.VMEM((total, inner), jnp.bfloat16),
            pltpu.SemaphoreType.DMA((2, SLOTS)),
            pltpu.SemaphoreType.DMA((wides,)),
        ],
        compiler_params=pltpu.CompilerParams(vmem_limit_bytes=LIMIT * 1024 * 1024),
        cost_estimate=pl.CostEstimate(
            flops=6 * total * width * inner,
            bytes_accessed=6 * width * inner,
            transcendentals=total * inner,
        ),
        name="expert_mlp",
    )(turns, weight, gate_w, up_w, down_w, *pieces, near, far)
    return outs[:8], outs[8], outs[9]


def body(acts, norm_gain, w_gate, w_up, w_down, routes, gates):
    gain = norm_gain[0]
    gate_w, up_w, down_w = w_gate[0, 0], w_up[0, 0], w_down[0, 0]
    rows, width = acts.shape[1:]
    me = lax.axis_index("expert")
    turns = jnp.stack([(me // 2 + dy) % 4 for dy in (0, 3, 1, 2)]).astype(jnp.int32)
    ids = jnp.arange(8, dtype=jnp.int32)
    chosen = (routes[:, 0, :, :, None] == ids).astype(jnp.float32)
    weights = jnp.sum(gates[:, 0, :, :, None] * chosen, axis=2)
    weights = jnp.transpose(weights, (1, 0, 2)).reshape(rows, TICKS * 8)
    riders = thirds(weights)
    columns = jnp.arange(TICKS * 8, dtype=jnp.int32)[None, :]
    first, second = acts[0, :, :FIRST], acts[0, :, FIRST:]
    for tick in range(TICKS):
        one, two = normalize(first, second, gain)
        if tick == 0:
            pieces, near, far = gather(one, jnp.concatenate([two, riders], axis=1))
            parts = jnp.stack([near[:, width - FIRST :], far[:, width - FIRST :]]).reshape(2, 4, rows, 128)
            weights = whole_again(jnp.swapaxes(parts, 0, 1).reshape(8 * rows, 128))
        else:
            pieces, near, far = gather(one, two)
        weight = jnp.sum(jnp.where(columns == tick * 8 + me, weights, 0.0), axis=1, keepdims=True)
        pieces, near, far = expert(turns, weight, gate_w, up_w, down_w, pieces, near, far)
        first, second = scatter_first(first, pieces), scatter_second(second, near, far)
    return jnp.concatenate([first, second], axis=1)[None]


def solution(mesh):
    return jax.shard_map(
        body,
        mesh=mesh,
        in_specs=(
            P("section", "expert", None),
            P("section", None),
            P("section", "expert", None, None),
            P("section", "expert", None, None),
            P("section", "expert", None, None),
            P(None, "section", "expert", None),
            P(None, "section", "expert", None),
        ),
        out_specs=P("section", "expert", None),
        check_vma=False,
    )
```

```python
import functools

import jax
import jax.numpy as jnp
from jax import lax
from jax.experimental import pallas as pl
from jax.experimental.pallas import tpu as pltpu
from jax.sharding import PartitionSpec as P

TICKS = 4
FIRST = 3584
DEEP = 1024
WIDE = 1024
SLOTS = 4
LIMIT = 40


def relayed(value, turn):
    pairs = []
    for s in range(16):
        for e in range(8):
            target = e ^ 1 if turn is None else (e + turn) % 8
            pairs.append((s * 8 + e, (s + 1) % 16 * 8 + target))
    return lax.ppermute(value, ("section", "expert"), pairs)


def across(value):
    return lax.ppermute(value, "expert", [(i, i ^ 1) for i in range(8)])


def upward(value):
    return lax.ppermute(value, "expert", [(i, (i + 2) % 8) for i in range(8)])


def downward(value):
    return lax.ppermute(value, "expert", [(i, (i - 2) % 8) for i in range(8)])


def plus(*terms):
    total = terms[0].astype(jnp.float32)
    for term in terms[1:]:
        total = total + term.astype(jnp.float32)
    return total


def normalize(first, second, gain):
    split = first.shape[1]
    one, two = first.astype(jnp.float32), second.astype(jnp.float32)
    total = jnp.sum(one * one, axis=-1, keepdims=True) + jnp.sum(two * two, axis=-1, keepdims=True)
    scale = lax.rsqrt(total / gain.shape[0] + 1e-05)
    one = (one * scale * gain[None, :split]).astype(jnp.bfloat16)
    two = (two * scale * gain[None, split:]).astype(jnp.bfloat16)
    return one, two


def thirds(weights):
    high = lax.reduce_precision(weights, 8, 7)
    rest = weights - high
    middle = lax.reduce_precision(rest, 8, 7)
    parts = jnp.concatenate([high, middle, rest - middle], axis=1)
    return jnp.pad(parts, ((0, 0), (0, 128 - parts.shape[1]))).astype(jnp.bfloat16)


def whole_again(parts):
    size = TICKS * 8
    high, middle, low = (parts[:, i * size : (i + 1) * size].astype(jnp.float32) for i in range(3))
    return high + (middle + low)


def gather(first, second):
    half, quarter = first.shape[1] // 2, second.shape[1] // 256 * 128
    other = across(first)
    below, above = upward(second), downward(second)
    own_l = jnp.concatenate([first[:, :half], other[:, :half]], axis=0)
    own_r = jnp.concatenate([first[:, half:], other[:, half:]], axis=0)
    below_l, above_r = upward(own_l), downward(own_r)
    below_r, above_l = upward(own_r), downward(own_l)
    facing = jnp.concatenate([upward(below[:, :quarter]), downward(above[:, quarter:])], axis=1)
    near = jnp.concatenate([second, below, above, facing], axis=0)
    far = across(after(near, other))
    opp_l, opp_r = upward(below_l), downward(above_r)
    return (own_l, own_r, below_l, below_r, above_l, above_r, opp_l, opp_r), near, far


def after(value, *others):
    return lax.optimization_barrier((value, *others))[0]


def scatter_first(first, pieces):
    own_l, own_r, below_l, below_r, above_l, above_r, opp_l, opp_r = pieces
    rows = first.shape[0]
    arrived_l, arrived_r = upward(opp_l), downward(opp_r)
    sum_r, sum_l = upward(above_r), downward(below_l)
    top_l = upward(plus(above_l, arrived_l).astype(jnp.bfloat16))
    low_r = downward(plus(below_r, arrived_r).astype(jnp.bfloat16))
    sums = jnp.concatenate([plus(own_l, sum_l, top_l), plus(own_r, sum_r, low_r)], axis=1)
    sent = relayed(sums[rows:].astype(jnp.bfloat16), None)
    kept = relayed((first.astype(jnp.float32) + sums[:rows]).astype(jnp.bfloat16), 0)
    return plus(kept, sent).astype(jnp.bfloat16)


def scatter_second(second, near, far):
    rows = second.shape[0]
    both = plus(near, across(far))
    kept = relayed((second.astype(jnp.float32) + both[:rows]).astype(jnp.bfloat16), 0)
    parts = [both[i * rows : (i + 1) * rows].astype(jnp.bfloat16) for i in (1, 2, 3)]
    sent = [relayed(part, turn) for part, turn in zip(parts, (-2, 2, 4))]
    return plus(kept, *sent).astype(jnp.bfloat16)


def mlp_kernel(weight, gate_hbm, up_hbm, down_hbm, *refs):
    pieces, (near, far) = refs[:8], refs[8:10]
    outs, (out_near, out_far) = refs[10:18], refs[18:20]
    block, gates, ups, downs, acc, hidden, in_sems, out_sems, row_sems, put_sems = refs[20:]
    pair, half = pieces[0].shape
    rows = pair // 2
    width, inner = gate_hbm.shape
    split = 2 * half
    steps, wides = width // DEEP, width // WIDE

    def fetch(at):
        slot, span = at % SLOTS, pl.ds(at * DEEP, DEEP)
        return (
            pltpu.make_async_copy(gate_hbm.at[span, :], gates.at[slot], in_sems.at[0, slot]),
            pltpu.make_async_copy(up_hbm.at[span, :], ups.at[slot], in_sems.at[1, slot]),
        )

    def fetch_down(at):
        return pltpu.make_async_copy(down_hbm.at[:, pl.ds(at * WIDE, WIDE)], downs.at[at], out_sems.at[at])

    def spots(firsts, seconds):
        for side in range(2):
            for dy in range(4):
                at = block.at[pl.ds(dy * pair, pair), pl.ds(side * half, half)]
                yield firsts[2 * dy + side], at, (side + 1) * half
        for dx, ref in enumerate(seconds):
            for dy in range(4):
                at = block.at[pl.ds((2 * dy + dx) * rows, rows), pl.ds(split, width - split)]
                yield ref.at[pl.ds(dy * rows, rows), pl.ds(0, width - split)], at, width

    arrivals = [
        (pltpu.make_async_copy(ref, at, row_sems.at[i]), end)
        for i, (ref, at, end) in enumerate(spots(pieces, (near, far)))
    ]
    departures = [
        (pltpu.make_async_copy(at, ref, put_sems.at[i]), end)
        for i, (ref, at, end) in enumerate(spots(outs, (out_near, out_far)))
    ]
    ends = (half, split, width)

    def within(start, stop):
        return [end for begin, end in zip((0, *ends), ends) if begin < stop and end > start]

    for copy, end in arrivals:
        if end == half:
            copy.start()
    for copy in fetch(0):
        copy.start()
    for copy, end in arrivals:
        if end > half:
            copy.start()
    for at in range(1, SLOTS):
        for copy in fetch(at):
            copy.start()
    here = set()
    for at in range(steps):
        for end in within(at * DEEP, (at + 1) * DEEP):
            if end not in here:
                here.add(end)
                for copy, of in arrivals:
                    if of == end:
                        copy.wait()
        for copy in fetch(at):
            copy.wait()
        lines = block[:, at * DEEP : (at + 1) * DEEP]
        for column, ref in ((0, gates), (inner, ups)):
            columns = slice(column, column + inner)
            part = jnp.dot(lines, ref[at % SLOTS], preferred_element_type=jnp.float32)
            acc[:, columns] = part if at == 0 else acc[:, columns] + part
        if at + SLOTS < steps:
            for copy in fetch(at + SLOTS):
                copy.start()
        elif at + SLOTS == steps:
            for wide in range(wides):
                fetch_down(wide).start()
    value = acc[:, :inner]
    hidden[...] = (value / (1.0 + jnp.exp(-value)) * acc[:, inner:] * weight[...]).astype(jnp.bfloat16)
    done = 0
    for at in range(wides):
        fetch_down(at).wait()
        output = jnp.dot(hidden[...], downs[at], preferred_element_type=jnp.float32)
        block[:, at * WIDE : (at + 1) * WIDE] = output.astype(jnp.bfloat16)
        for copy, end in departures:
            if done < end <= (at + 1) * WIDE:
                copy.start()
        done = (at + 1) * WIDE
    for copy, _ in departures:
        copy.wait()


def expert(weight, gate_w, up_w, down_w, pieces, near, far):
    width, inner = gate_w.shape
    pair, half = pieces[0].shape
    total = pair * 4
    wides = width // WIDE
    mixed = (2 * pair, width - 2 * half)
    anywhere = pl.BlockSpec(memory_space=pl.ANY)
    outs = pl.pallas_call(
        mlp_kernel,
        in_specs=[pl.BlockSpec(memory_space=pltpu.VMEM)] + [anywhere] * 13,
        out_specs=[anywhere] * 10,
        out_shape=[jax.ShapeDtypeStruct((pair, half), jnp.bfloat16)] * 8
        + [jax.ShapeDtypeStruct(mixed, jnp.bfloat16)] * 2,
        scratch_shapes=[
            pltpu.VMEM((total, width), jnp.bfloat16),
            pltpu.VMEM((SLOTS, DEEP, inner), jnp.bfloat16),
            pltpu.VMEM((SLOTS, DEEP, inner), jnp.bfloat16),
            pltpu.VMEM((wides, inner, WIDE), jnp.bfloat16),
            pltpu.VMEM((total, 2 * inner), jnp.float32),
            pltpu.VMEM((total, inner), jnp.bfloat16),
            pltpu.SemaphoreType.DMA((2, SLOTS)),
            pltpu.SemaphoreType.DMA((wides,)),
            pltpu.SemaphoreType.DMA((16,)),
            pltpu.SemaphoreType.DMA((16,)),
        ],
        compiler_params=pltpu.CompilerParams(vmem_limit_bytes=LIMIT * 1024 * 1024),
        cost_estimate=pl.CostEstimate(
            flops=6 * total * width * inner,
            bytes_accessed=6 * width * inner,
            transcendentals=total * inner,
        ),
        name="expert_mlp",
    )(weight, gate_w, up_w, down_w, *pieces, near, far)
    return outs[:8], outs[8], outs[9]


def body(acts, norm_gain, w_gate, w_up, w_down, routes, gates):
    gain = norm_gain[0]
    gate_w, up_w, down_w = w_gate[0, 0], w_up[0, 0], w_down[0, 0]
    rows, width = acts.shape[1:]
    me = lax.axis_index("expert")
    ids = jnp.arange(8, dtype=jnp.int32)
    chosen = (routes[:, 0, :, :, None] == ids).astype(jnp.float32)
    weights = jnp.sum(gates[:, 0, :, :, None] * chosen, axis=2)
    weights = jnp.transpose(weights, (1, 0, 2)).reshape(rows, TICKS * 8)
    riders = thirds(weights)
    columns = jnp.arange(TICKS * 8, dtype=jnp.int32)[None, :]
    first, second = acts[0, :, :FIRST], acts[0, :, FIRST:]
    for tick in range(TICKS):
        one, two = normalize(first, second, gain)
        if tick == 0:
            pieces, near, far = gather(one, jnp.concatenate([two, riders], axis=1))
            parts = jnp.stack([near[:, width - FIRST :], far[:, width - FIRST :]]).reshape(2, 4, rows, 128)
            weights = whole_again(jnp.swapaxes(parts, 0, 1).reshape(8 * rows, 128))
        else:
            pieces, near, far = gather(one, two)
        weight = jnp.sum(jnp.where(columns == tick * 8 + me, weights, 0.0), axis=1, keepdims=True)
        pieces, near, far = expert(weight, gate_w, up_w, down_w, pieces, near, far)
        first, second = scatter_first(first, pieces), scatter_second(second, near, far)
    return jnp.concatenate([first, second], axis=1)[None]


def solution(mesh):
    return jax.shard_map(
        body,
        mesh=mesh,
        in_specs=(
            P("section", "expert", None),
            P("section", None),
            P("section", "expert", None, None),
            P("section", "expert", None, None),
            P("section", "expert", None, None),
            P(None, "section", "expert", None),
            P(None, "section", "expert", None),
        ),
        out_specs=P("section", "expert", None),
        check_vma=False,
    )
```

```python
import functools

import jax
import jax.numpy as jnp
from jax import lax
from jax.experimental import pallas as pl
from jax.experimental.pallas import tpu as pltpu
from jax.sharding import PartitionSpec as P

TICKS = 4
FIRST = 3584
DEEP = 1024
WIDE = 1024
SLOTS = 4
LIMIT = 40


def relayed(value, turn):
    pairs = []
    for s in range(16):
        for e in range(8):
            target = e ^ 1 if turn is None else (e + turn) % 8
            pairs.append((s * 8 + e, (s + 1) % 16 * 8 + target))
    return lax.ppermute(value, ("section", "expert"), pairs)


def across(value):
    return lax.ppermute(value, "expert", [(i, i ^ 1) for i in range(8)])


def upward(value):
    return lax.ppermute(value, "expert", [(i, (i + 2) % 8) for i in range(8)])


def downward(value):
    return lax.ppermute(value, "expert", [(i, (i - 2) % 8) for i in range(8)])


def plus(*terms):
    total = terms[0].astype(jnp.float32)
    for term in terms[1:]:
        total = total + term.astype(jnp.float32)
    return total


def normalize(first, second, gain):
    split = first.shape[1]
    one, two = first.astype(jnp.float32), second.astype(jnp.float32)
    total = jnp.sum(one * one, axis=-1, keepdims=True) + jnp.sum(two * two, axis=-1, keepdims=True)
    scale = lax.rsqrt(total / gain.shape[0] + 1e-05)
    one = (one * scale * gain[None, :split]).astype(jnp.bfloat16)
    two = (two * scale * gain[None, split:]).astype(jnp.bfloat16)
    return one, two


def thirds(weights):
    high = lax.reduce_precision(weights, 8, 7)
    rest = weights - high
    middle = lax.reduce_precision(rest, 8, 7)
    parts = jnp.concatenate([high, middle, rest - middle], axis=1)
    return jnp.pad(parts, ((0, 0), (0, 128 - parts.shape[1]))).astype(jnp.bfloat16)


def whole_again(parts):
    size = TICKS * 8
    high, middle, low = (parts[:, i * size : (i + 1) * size].astype(jnp.float32) for i in range(3))
    return high + (middle + low)


def gather(first, second):
    half, quarter = first.shape[1] // 2, second.shape[1] // 256 * 128
    other = across(first)
    below, above = upward(second), downward(second)
    own_l = jnp.concatenate([first[:, :half], other[:, :half]], axis=0)
    own_r = jnp.concatenate([first[:, half:], other[:, half:]], axis=0)
    below_l, above_r = upward(own_l), downward(own_r)
    below_r, above_l = upward(own_r), downward(own_l)
    facing = jnp.concatenate([upward(below[:, :quarter]), downward(above[:, quarter:])], axis=1)
    near = jnp.concatenate([second, below, above, facing], axis=0)
    far = across(after(near, other))
    opp_l, opp_r = upward(below_l), downward(above_r)
    return (own_l, own_r, below_l, below_r, above_l, above_r, opp_l, opp_r), near, far


def after(value, *others):
    return lax.optimization_barrier((value, *others))[0]


def scatter_sum(first, second, pieces, near, far):
    own_l, own_r, below_l, below_r, above_l, above_r, opp_l, opp_r = pieces
    rows, split = first.shape
    other = across(far)
    arrived_l, arrived_r = upward(opp_l), downward(opp_r)
    sum_r, sum_l = upward(above_r), downward(below_l)
    top_l = upward(plus(above_l, arrived_l).astype(jnp.bfloat16))
    low_r = downward(plus(below_r, arrived_r).astype(jnp.bfloat16))
    both = plus(near, other)
    parts = [both[i * rows : (i + 1) * rows].astype(jnp.bfloat16) for i in (1, 2, 3)]
    more = [relayed(part, turn) for part, turn in zip(parts, (-2, 2, 4))]
    sums = jnp.concatenate([plus(own_l, sum_l, top_l), plus(own_r, sum_r, low_r)], axis=1)
    sent = relayed(sums[rows:].astype(jnp.bfloat16), None)
    home = jnp.concatenate([first.astype(jnp.float32) + sums[:rows], second.astype(jnp.float32) + both[:rows]], axis=1)
    kept = relayed(home.astype(jnp.bfloat16), 0)
    first = plus(kept[:, :split], sent).astype(jnp.bfloat16)
    return first, plus(kept[:, split:], *more).astype(jnp.bfloat16)


def mlp_kernel(weight, gate_hbm, up_hbm, down_hbm, *refs):
    pieces, (near, far) = refs[:8], refs[8:10]
    outs, (out_near, out_far) = refs[10:18], refs[18:20]
    block, gates, ups, downs, acc, hidden, in_sems, out_sems, row_sems, put_sems = refs[20:]
    pair, half = pieces[0].shape
    rows = pair // 2
    width, inner = gate_hbm.shape
    split = 2 * half
    steps, wides = width // DEEP, width // WIDE

    def fetch(at):
        slot, span = at % SLOTS, pl.ds(at * DEEP, DEEP)
        return (
            pltpu.make_async_copy(gate_hbm.at[span, :], gates.at[slot], in_sems.at[0, slot]),
            pltpu.make_async_copy(up_hbm.at[span, :], ups.at[slot], in_sems.at[1, slot]),
        )

    def fetch_down(at):
        return pltpu.make_async_copy(down_hbm.at[:, pl.ds(at * WIDE, WIDE)], downs.at[at], out_sems.at[at])

    def spots(firsts, seconds):
        for side in range(2):
            for dy in range(4):
                at = block.at[pl.ds(dy * pair, pair), pl.ds(side * half, half)]
                yield firsts[2 * dy + side], at, (side + 1) * half
        for dx, ref in enumerate(seconds):
            for dy in range(4):
                at = block.at[pl.ds((2 * dy + dx) * rows, rows), pl.ds(split, width - split)]
                yield ref.at[pl.ds(dy * rows, rows), pl.ds(0, width - split)], at, width

    arrivals = [
        (pltpu.make_async_copy(ref, at, row_sems.at[i]), end)
        for i, (ref, at, end) in enumerate(spots(pieces, (near, far)))
    ]
    departures = [
        (pltpu.make_async_copy(at, ref, put_sems.at[i]), end)
        for i, (ref, at, end) in enumerate(spots(outs, (out_near, out_far)))
    ]
    ends = (half, split, width)

    def within(start, stop):
        return [end for begin, end in zip((0, *ends), ends) if begin < stop and end > start]

    for copy, end in arrivals:
        if end == half:
            copy.start()
    for copy in fetch(0):
        copy.start()
    for copy, end in arrivals:
        if end > half:
            copy.start()
    for at in range(1, SLOTS):
        for copy in fetch(at):
            copy.start()
    here = set()
    for at in range(steps):
        for end in within(at * DEEP, (at + 1) * DEEP):
            if end not in here:
                here.add(end)
                for copy, of in arrivals:
                    if of == end:
                        copy.wait()
        for copy in fetch(at):
            copy.wait()
        lines = block[:, at * DEEP : (at + 1) * DEEP]
        for column, ref in ((0, gates), (inner, ups)):
            columns = slice(column, column + inner)
            part = jnp.dot(lines, ref[at % SLOTS], preferred_element_type=jnp.float32)
            acc[:, columns] = part if at == 0 else acc[:, columns] + part
        if at + SLOTS < steps:
            for copy in fetch(at + SLOTS):
                copy.start()
        elif at + SLOTS == steps:
            for wide in range(wides):
                fetch_down(wide).start()
    value = acc[:, :inner]
    hidden[...] = (value / (1.0 + jnp.exp(-value)) * acc[:, inner:] * weight[...]).astype(jnp.bfloat16)
    done = 0
    for at in range(wides):
        fetch_down(at).wait()
        output = jnp.dot(hidden[...], downs[at], preferred_element_type=jnp.float32)
        block[:, at * WIDE : (at + 1) * WIDE] = output.astype(jnp.bfloat16)
        for copy, end in departures:
            if done < end <= (at + 1) * WIDE:
                copy.start()
        done = (at + 1) * WIDE
    for copy, _ in departures:
        copy.wait()


def expert(weight, gate_w, up_w, down_w, pieces, near, far):
    width, inner = gate_w.shape
    pair, half = pieces[0].shape
    total = pair * 4
    wides = width // WIDE
    mixed = (2 * pair, width - 2 * half)
    anywhere = pl.BlockSpec(memory_space=pl.ANY)
    outs = pl.pallas_call(
        mlp_kernel,
        in_specs=[pl.BlockSpec(memory_space=pltpu.VMEM)] + [anywhere] * 13,
        out_specs=[anywhere] * 10,
        out_shape=[jax.ShapeDtypeStruct((pair, half), jnp.bfloat16)] * 8
        + [jax.ShapeDtypeStruct(mixed, jnp.bfloat16)] * 2,
        scratch_shapes=[
            pltpu.VMEM((total, width), jnp.bfloat16),
            pltpu.VMEM((SLOTS, DEEP, inner), jnp.bfloat16),
            pltpu.VMEM((SLOTS, DEEP, inner), jnp.bfloat16),
            pltpu.VMEM((wides, inner, WIDE), jnp.bfloat16),
            pltpu.VMEM((total, 2 * inner), jnp.float32),
            pltpu.VMEM((total, inner), jnp.bfloat16),
            pltpu.SemaphoreType.DMA((2, SLOTS)),
            pltpu.SemaphoreType.DMA((wides,)),
            pltpu.SemaphoreType.DMA((16,)),
            pltpu.SemaphoreType.DMA((16,)),
        ],
        compiler_params=pltpu.CompilerParams(vmem_limit_bytes=LIMIT * 1024 * 1024),
        cost_estimate=pl.CostEstimate(
            flops=6 * total * width * inner,
            bytes_accessed=6 * width * inner,
            transcendentals=total * inner,
        ),
        name="expert_mlp",
    )(weight, gate_w, up_w, down_w, *pieces, near, far)
    return outs[:8], outs[8], outs[9]


def body(acts, norm_gain, w_gate, w_up, w_down, routes, gates):
    gain = norm_gain[0]
    gate_w, up_w, down_w = w_gate[0, 0], w_up[0, 0], w_down[0, 0]
    rows, width = acts.shape[1:]
    me = lax.axis_index("expert")
    ids = jnp.arange(8, dtype=jnp.int32)
    chosen = (routes[:, 0, :, :, None] == ids).astype(jnp.float32)
    weights = jnp.sum(gates[:, 0, :, :, None] * chosen, axis=2)
    weights = jnp.transpose(weights, (1, 0, 2)).reshape(rows, TICKS * 8)
    riders = thirds(weights)
    columns = jnp.arange(TICKS * 8, dtype=jnp.int32)[None, :]
    first, second = acts[0, :, :FIRST], acts[0, :, FIRST:]
    for tick in range(TICKS):
        one, two = normalize(first, second, gain)
        if tick == 0:
            pieces, near, far = gather(one, jnp.concatenate([two, riders], axis=1))
            parts = jnp.stack([near[:, width - FIRST :], far[:, width - FIRST :]]).reshape(2, 4, rows, 128)
            weights = whole_again(jnp.swapaxes(parts, 0, 1).reshape(8 * rows, 128))
        else:
            pieces, near, far = gather(one, two)
        weight = jnp.sum(jnp.where(columns == tick * 8 + me, weights, 0.0), axis=1, keepdims=True)
        pieces, near, far = expert(weight, gate_w, up_w, down_w, pieces, near, far)
        first, second = scatter_sum(first, second, pieces, near, far)
    return jnp.concatenate([first, second], axis=1)[None]


def solution(mesh):
    return jax.shard_map(
        body,
        mesh=mesh,
        in_specs=(
            P("section", "expert", None),
            P("section", None),
            P("section", "expert", None, None),
            P("section", "expert", None, None),
            P("section", "expert", None, None),
            P(None, "section", "expert", None),
            P(None, "section", "expert", None),
        ),
        out_specs=P("section", "expert", None),
        check_vma=False,
    )
```
